256 devices in a mesh: dp: 8 (over x, core), tensor: 32 (over y, z).
Axes of the slice: x: 4, y: 4, z: 8, core: 2. Of those that a mesh axis runs over, the one named last changes fastest.
Arguments:
- out_grad: bfloat16 [1024, 16384], P('tensor', 'dp'), may hold values from -6 to 6
- down_weight: bfloat16 [53248, 16384], P('tensor', 'dp'), may hold values from -0.046875 to 0.046875
- gate_pre: bfloat16 [1024, 53248], P('dp', 'tensor'), may hold values from -6 to 6
- inputs: bfloat16 [1024, 16384], P('dp', 'tensor'), may hold values from -6 to 6
- test_matrix: bfloat16 [53248, 128], P('tensor'), may hold values from -0.02734375 to 0.02734375
Outputs:
- basis: float32 [16384, 128], P('tensor')
- corange: float32 [128, 53248], P(None, 'tensor')
The draws below stay inside these ranges and needn't reach their ends.
All inputs are finite; a program needn't handle non-finite values.
Results may differ from the reference program's by a relative error of at most 0.0044.
Values may be sent and summed in bfloat16 or wider, within the bound.
A program may use at most 64 MiB of HBM per device.

```python
import math
import jax
import jax.numpy as jnp
from jax import lax

D = 16384
FF = 53248
R = 128
TOKENS = 1024


def steps_of(rng, shape, pieces, least, high):
    def one(axis_at, blocks):
        steps = jax.random.uniform(jax.random.fold_in(jax.random.fold_in(rng, 6), axis_at), (blocks,), jnp.float32, least / len(pieces), high / len(pieces))
        return jnp.repeat(jnp.exp(steps), shape[axis_at] // blocks).reshape((-1,) + (1,) * (len(shape) - axis_at - 1))

    level = one(*pieces[0])
    for cut in pieces[1:]:
        level = level * one(*cut)
    return level


def scatter_about(own_key, extent, deviation, limit, shards=(), dtype=jnp.bfloat16):
    entries = deviation * jax.random.normal(own_key, extent, jnp.float32)
    if shards:
        entries = entries * steps_of(own_key, extent, shards, -0.22, 0.18)
    return jnp.clip(entries, -limit, limit).astype(dtype)


def setup_inputs(seed: int = 0) -> dict:
    splits = jax.random.split(jax.random.key(seed), 6)
    return {
        "out_grad": scatter_about(splits[0], (TOKENS, D), 1.0, 6.0, ((0, 32), (1, 8))),
        "down_weight": scatter_about(splits[1], (FF, D), D ** -0.5, 0.046875, ((0, 32), (1, 8))),
        "gate_pre": scatter_about(splits[2], (TOKENS, FF), 1.0, 6.0, ((0, 8), (1, 32))),
        "inputs": scatter_about(splits[3], (TOKENS, D), 1.0, 6.0, ((0, 8), (1, 32))),
        "test_matrix": scatter_about(splits[4], (FF, R), FF ** -0.5, 0.02734375, ((0, 32),)),
    }


def reference(out_grad, down_weight, gate_pre, inputs, test_matrix):
    hidden_grad = lax.dot_general(out_grad.astype(jnp.float32), down_weight.astype(jnp.float32), (((1,), (1,)), ((), ())), preferred_element_type=jnp.float32)
    up_grad = (hidden_grad * jax.nn.silu(gate_pre.astype(jnp.float32))).astype(jnp.bfloat16)
    sketch = jnp.dot(up_grad.astype(jnp.float32), test_matrix.astype(jnp.float32), preferred_element_type=jnp.float32)
    factor = 1.0 / math.sqrt(TOKENS)
    inputs_wide = inputs.astype(jnp.float32)
    range_cols = lax.dot_general(inputs_wide, sketch, (((0,), (0,)), ((), ())), precision=lax.Precision.HIGHEST) * factor
    gram = jnp.dot(range_cols.T, range_cols, precision=lax.Precision.HIGHEST)
    lower = jnp.linalg.cholesky(gram)
    ortho = lax.linalg.triangular_solve(lower, range_cols, left_side=False, lower=True, transpose_a=True)
    basis = ortho * math.sqrt(D)
    coeff = jnp.dot(inputs_wide, ortho, precision=lax.Precision.HIGHEST)
    corange = lax.dot_general(coeff, up_grad.astype(jnp.float32), (((0,), (0,)), ((), ())), precision=lax.Precision.HIGHEST) * factor
    return (basis, corange)
```

```python
import functools
import math

import jax
import jax.numpy as jnp
from jax import lax
from jax.experimental import pallas as pl
from jax.experimental.pallas import tpu as pltpu
from jax.sharding import PartitionSpec as P

MESH = pl.DeviceIdType.MESH
F32 = jnp.float32
BF16 = jnp.bfloat16

NX, NC, NY, NZ = 4, 2, 4, 8
CUT = 896
LAST = 2 * (NZ // 2) - 1


def slot_from_below(k):
    return LAST if k == NZ // 2 else 2 * k


def slot_from_above(k):
    return LAST if k == NZ // 2 else 2 * k - 1


OFFSET = {0: 0, LAST: NZ // 2}
for _k in range(1, NZ // 2):
    OFFSET[slot_from_below(_k)] = NZ - _k
    OFFSET[slot_from_above(_k)] = _k


def split3(v):
    hi = v.astype(BF16)
    rest = v - hi.astype(F32)
    mid = rest.astype(BF16)
    low = (rest - mid.astype(F32)).astype(BF16)
    return hi, mid, low


def dot(a, b, ca, cb, precision=None):
    return lax.dot_general(
        a, b, (((ca,), (cb,)), ((), ())), preferred_element_type=F32, precision=precision
    )


HIGHEST = lax.Precision.HIGHEST


def inverse_factor(gram, work):
    n = gram.shape[0]
    ri = lax.broadcasted_iota(jnp.int32, (n, n), 0)
    ci = lax.broadcasted_iota(jnp.int32, (n, n), 1)
    work[:, :n] = gram
    work[:, n:] = jnp.where(ri == ci, 1.0, 0.0).astype(F32)
    sub = lax.broadcasted_iota(jnp.int32, (8, n), 0)
    sub2 = lax.broadcasted_iota(jnp.int32, (8, 2 * n), 0)
    for b in range(n // 8):
        rows = slice(8 * b, 8 * b + 8)
        panel = work[rows, :]
        cols = [
            jnp.broadcast_to(panel[:, 8 * b + m : 8 * b + m + 1], (8, n)) for m in range(8)
        ]
        for k in range(8):
            inv = lax.rsqrt(cols[k][k : k + 1, :])
            fac = jnp.where(sub > k, cols[k] * inv, 0.0)
            fac2 = jnp.concatenate([fac, fac], axis=1)
            inv2 = jnp.concatenate([inv, inv], axis=1)
            row = panel[k : k + 1, :] * inv2
            panel = jnp.where(sub2 == k, row, panel - fac2 * row)
            for m in range(k + 1, 8):
                cols[m] = cols[m] - fac * (cols[m][k : k + 1, :] * inv)
        work[rows, :] = panel
        done = 8 * (b + 1)
        if done < n:
            hi = panel.astype(BF16).astype(F32)
            mid = (panel - hi).astype(BF16).astype(F32)
            low = panel - hi - mid
            left = jnp.concatenate([hi, hi, mid, hi, low, mid], axis=0)[:, :n].astype(BF16)
            right = jnp.concatenate([hi, mid, hi, low, hi, mid], axis=0).astype(BF16)
            work[done:, :] = work[done:, :] - dot(left, right, 0, 0)[done:, :]


def kernel(
    og, dw, gate, inp, test, basis, corange,
    G, W, GT, XB, TM, SIL, PT, SIBR, SIB0, HG, FS, FR, XS, RX, U, XT,
    SP, S1, S2, SF, V, V1, V2, VF, WK, M, MS, MC, MR, MF,
    sends, recvs, local,
):
    d, t = lax.axis_index("dp"), lax.axis_index("tensor")
    x, c = d // NC, lax.rem(d, NC)
    y, z = t // NZ, lax.rem(t, NZ)
    tokens = NX * NC * XB.shape[1]
    factor = 1.0 / math.sqrt(tokens)
    features = inp.shape[1] * NY * NZ

    def mod(a, n):
        return lax.rem(a + n, n)

    def at_yz(yy, zz):
        return {"dp": d, "tensor": yy * NZ + zz}

    def at_xc(xx, cc):
        return {"dp": xx * NC + cc, "tensor": t}

    zu, zd = at_yz(y, mod(z + 1, NZ)), at_yz(y, mod(z - 1, NZ))
    yu, yd, y2 = at_yz(mod(y + 1, NY), z), at_yz(mod(y - 1, NY), z), at_yz(mod(y + 2, NY), z)
    xu, xd = mod(x + 1, NX), mod(x - 1, NX)
    twin = at_xc(x, 1 - c)

    pending = []
    count = {"s": 0, "r": 0}

    def take_recv(n):
        base = count["r"]
        count["r"] += n
        return base

    def send(src, dst, recv, dev, when=None):
        idx = count["s"]
        count["s"] += 1
        cp = pltpu.make_async_remote_copy(
            src_ref=src, dst_ref=dst, send_sem=sends.at[idx], recv_sem=recvs.at[recv],
            device_id=dev, device_id_type=MESH,
        )
        if when is None:
            cp.start()
        else:
            pl.when(when)(cp.start)
        pending.append((cp, when))

    def arrive(ref, recv):
        pltpu.make_async_remote_copy(
            src_ref=ref, dst_ref=ref, send_sem=sends.at[0], recv_sem=recvs.at[recv],
            device_id=twin, device_id_type=MESH,
        ).wait_recv()

    q0, qp, qn, q2 = mod(y - x, NY), mod(y - 1 - x, NY), mod(y + 1 - x, NY), mod(y + 2 - x, NY)

    half = og.shape[0] // 2
    loads = [
        pltpu.make_async_copy(og.at[pl.ds(0, half)], G.at[q0 * 2], local.at[0]),
        pltpu.make_async_copy(og.at[pl.ds(half, half)], G.at[q0 * 2 + 1], local.at[1]),
        pltpu.make_async_copy(inp, XB.at[d], local.at[2]),
        pltpu.make_async_copy(dw, W, local.at[3]),
        pltpu.make_async_copy(gate, GT, local.at[4]),
        pltpu.make_async_copy(test, TM, local.at[5]),
    ]
    for cp in loads:
        cp.start()

    barrier = pltpu.get_barrier_semaphore()
    peers = [at_yz(y, mod(z + o, NZ)) for o in range(1, NZ)]
    peers += [yu, yd, y2]
    peers += [at_xc(mod(x + o, NX), cc) for o in range(1, NX) for cc in range(NC)] + [twin]
    for dev in peers:
        pl.semaphore_signal(barrier, inc=1, device_id=dev, device_id_type=MESH)
    pl.semaphore_wait(barrier, len(peers))
    loads[0].wait()
    loads[1].wait()

    ag = take_recv(8 * NY * 2)

    def item(slot, q, h):
        return (slot * NY + q) * 2 + h

    def pass_on(slot, q, h, to_slot, dev, when=None):
        send(G.at[item(slot, q, h)], G.at[item(to_slot, q, h)], ag + item(to_slot, q, h), dev, when)

    def got(slot, q, h):
        arrive(G.at[item(slot, q, h)], ag + item(slot, q, h))

    below, above = slot_from_below, slot_from_above
    TOP = NZ // 2

    pass_on(0, q0, 1, 0, yu)
    pass_on(0, q0, 1, 0, yd)
    pass_on(0, q0, 0, below(1), zu)
    pass_on(0, q0, 0, above(1), zd)
    pass_on(0, q0, 1, 0, y2)
    pass_on(0, q0, 0, 0, yu)
    pass_on(0, q0, 0, 0, yd)

    loads[2].wait()
    xr = take_recv(NX * NC)
    for o in (1, 3, 2):
        send(XB.at[d], XB.at[d], xr + d, at_xc(mod(x + o, NX), c))
    send(XB.at[d], XB.at[d], xr + d, twin)

    def first_half_from_z(k):
        if k < TOP:
            s = above(k)
            got(s, q0, 0)
            if k + 1 < TOP:
                pass_on(s, q0, 0, above(k + 1), zd)
            pass_on(s, q0, 0, s, yu)
            pass_on(s, q0, 0, s, yd)
        s = below(k)
        got(s, q0, 0)
        if k < TOP:
            pass_on(s, q0, 0, below(k + 1), zu)
        pass_on(s, q0, 0, s, yu)
        pass_on(s, q0, 0, s, yd)

    def first_half_from_y(s):
        got(s, qp, 0)
        if s % 2 == 0:
            pass_on(s, qp, 0, s, yu)
        got(s, qn, 0)
        if s % 2 == 1:
            pass_on(s, qn, 0, s, yd)

    def on_along_z(q):
        pass_on(0, q, 1, below(1), zu)
        pass_on(0, q, 1, above(1), zd)

    sibs = take_recv(24)
    sib0 = take_recv(4)
    fw = take_recv(16)
    rx = take_recv(16)
    n = W.shape[0]
    WIDE = 256

    def column(s):
        return lax.rem(z + OFFSET[s], NZ)

    def product(s0, slots):
        i0, ni = s0 * NY * 2, slots * NY * 2
        rows = ni * half

        def cols_at(start, width):
            a = G[pl.ds(i0, ni)].reshape(rows, G.shape[2])
            b = W[pl.ds(start, width), :]
            PT[pl.ds(i0, ni), :, pl.ds(start, width)] = dot(a, b, 1, 1).reshape(ni, half, width)

        def body(j, _):
            cols_at(pl.multiple_of(j * WIDE, WIDE), WIDE)
            return 0

        lax.fori_loop(0, n // WIDE, body, 0)
        if n % WIDE:
            cols_at(n - n % WIDE, n % WIDE)

    def exchange(s):
        owner = column(s) // (NZ // NC)
        zc = lax.rem(column(s), NZ // NC)
        for q in range(1, NX):
            send(
                PT.at[item(s, q, 1 - c)], SIBR.at[s, q - 1], sibs + s * 3 + q - 1, twin
            )
        send(PT.at[pl.ds(item(s, 0, 0), 2)], SIB0.at[zc], sib0 + zc, twin, owner != c)

        @pl.when(owner == c)
        def _():
            HG[zc] = PT[pl.ds(item(s, 0, 0), 2)]

    def two_hops(s):
        arrive(SIBR.at[s, 1], sibs + s * 3 + 1)
        FS[s] = (PT[item(s, 2, c)] + SIBR[s, 1]).astype(BF16)
        send(FS.at[s, :, pl.ds(0, CUT)], FR.at[s, :, pl.ds(0, CUT)], fw + 2 * s, at_xc(xu, c))
        send(
            FS.at[s, :, pl.ds(CUT, n - CUT)], FR.at[s, :, pl.ds(CUT, n - CUT)],
            fw + 2 * s + 1, at_xc(xd, c),
        )

    def one_hop(s):
        owner = column(s) // (NZ // NC)
        zc = lax.rem(column(s), NZ // NC)
        arrive(SIBR.at[s, 0], sibs + s * 3)
        arrive(SIBR.at[s, 2], sibs + s * 3 + 2)
        arrive(FR.at[s, :, pl.ds(0, CUT)], fw + 2 * s)
        v = PT[item(s, 1, c)] + SIBR[s, 0]
        XS[s, 0, :, :CUT] = (v[:, :CUT] + FR[s, :, :CUT].astype(F32)).astype(BF16)
        XS[s, 0, :, CUT:] = v[:, CUT:].astype(BF16)
        k = (zc * 2 + c) * 2
        send(XS.at[s, 0], RX.at[0, zc, c], rx + k, at_xc(xu, owner))
        arrive(FR.at[s, :, pl.ds(CUT, n - CUT)], fw + 2 * s + 1)
        v = PT[item(s, 3, c)] + SIBR[s, 2]
        XS[s, 1, :, :CUT] = v[:, :CUT].astype(BF16)
        XS[s, 1, :, CUT:] = (v[:, CUT:] + FR[s, :, CUT:].astype(F32)).astype(BF16)
        send(XS.at[s, 1], RX.at[1, zc, c], rx + k + 1, at_xc(xd, owner))

    groups = [[0]] + [[above(k), below(k)] for k in range(1, TOP)] + [[LAST]]

    first_half_from_z(1)
    on_along_z(q0)
    for q in (qp, qn, q2):
        got(0, q, 1)
        on_along_z(q)
    first_half_from_y(0)
    got(0, q2, 0)
    loads[3].wait()
    product(0, 1)
    for s in groups[0]:
        exchange(s)
    for k in range(1, TOP + 1):
        if k < TOP:
            first_half_from_z(k + 1)
            for q in range(NY):
                got(above(k), q, 1)
                if k + 1 < TOP or q >= 2:
                    pass_on(above(k), q, 1, above(k + 1), zd)
                got(below(k), q, 1)
                if k + 1 < TOP or q < 2:
                    pass_on(below(k), q, 1, below(k + 1), zu)
        else:
            for q in range(NY):
                got(LAST, q, 1)
        if k == 1:
            loads[4].wait()
            g = GT[...].astype(F32)
            SIL[...] = g * (1.0 / (1.0 + jnp.exp(-g)))
            for o in (1, 3, 2):
                e = mod(x + o, NX) * NC + c
                arrive(XB.at[e], xr + e)
                send(XB.at[e], XB.at[e], xr + e, twin)
        if k == 2:
            for o in range(NX):
                e = mod(x + o, NX) * NC + 1 - c
                arrive(XB.at[e], xr + e)
            rows = XB.shape[1]
            for e in range(NX * NC):
                XT[:, e * rows : (e + 1) * rows] = XB[e].T
        for s in groups[k]:
            first_half_from_y(s)
        for s in groups[k]:
            got(s, q2, 0)
        product(groups[k][0], len(groups[k]))
        for s in groups[k]:
            exchange(s)
        for s in groups[k - 1]:
            two_hops(s)
        if k >= 2:
            for s in groups[k - 2]:
                one_hop(s)
    for s in groups[TOP]:
        two_hops(s)
    for s in groups[TOP - 1]:
        one_hop(s)
    for s in groups[TOP]:
        one_hop(s)

    loads[5].wait()
    for zc in range(NZ // NC):
        arrive(SIB0.at[zc], sib0 + zc)
        for h in range(2):
            arrive(RX.at[0, zc, h], rx + (zc * 2 + h) * 2)
            arrive(RX.at[1, zc, h], rx + (zc * 2 + h) * 2 + 1)
            v = (HG[zc, h] + SIB0[zc, h]) + (
                RX[0, zc, h].astype(F32) + RX[1, zc, h].astype(F32)
            )
            rows = slice((zc * 2 + h) * half, (zc * 2 + h + 1) * half)
            U[rows, :] = (v * SIL[rows, :]).astype(BF16)

    r = TM.shape[1]
    part = r // NZ
    own = XB.shape[1]

    def over_tensor(src, first, second, full, place):
        r1, r2, r3 = take_recv(NZ), take_recv(NY), take_recv(NZ)
        first[z] = src[z]
        for o in (4, 3, 5, 2, 6, 1, 7):
            zz = mod(z + o, NZ)
            send(src.at[zz], first.at[z], r1 + z, at_yz(y, zz))
        for o in (1, 7, 2, 6, 3, 5, 4):
            zz = mod(z + o, NZ)
            arrive(first.at[zz], r1 + zz)
        v = first[0]
        for j in range(1, NZ):
            v = v + first[j]
        second[y] = v
        for o in (2, 1, 3):
            send(second.at[y], second.at[y], r2 + y, at_yz(mod(y + o, NY), z))
        for o in (1, 3, 2):
            yy = mod(y + o, NY)
            arrive(second.at[yy], r2 + yy)
        v = second[0]
        for j in range(1, NY):
            v = v + second[j]
        place(z, v)
        for o in (4, 3, 5, 2, 6, 1, 7):
            send(full(z), full(z), r3 + z, at_yz(y, mod(z + o, NZ)))
        for o in (1, 7, 2, 6, 3, 5, 4):
            zz = mod(z + o, NZ)
            arrive(full(zz), r3 + zz)

    def over_dp(full):
        r1 = take_recv(NX * NC)
        for o in (2, 1, 3):
            send(full(d), full(d), r1 + d, at_xc(mod(x + o, NX), c))
        send(full(d), full(d), r1 + d, twin)
        for o in (1, 3, 2):
            e = mod(x + o, NX) * NC + c
            arrive(full(e), r1 + e)
            send(full(e), full(e), r1 + e, twin)
        for o in range(NX):
            e = mod(x + o, NX) * NC + 1 - c
            arrive(full(e), r1 + e)

    SP[...] = dot(U[...], TM[...], 1, 0).reshape(NZ, part, r)

    def place_s(zz, v):
        SF[d, zz] = v

    over_tensor(SP, S1, S2, lambda zz: SF.at[d, zz], place_s)
    over_dp(lambda e: SF.at[e])

    s = SF[...].reshape(tokens, r)
    rc = jnp.zeros((XT.shape[0], r), F32)
    xt = XT[...]
    for piece in split3(s)[::-1]:
        rc = rc + dot(xt, piece, 1, 0)
    rc = rc * factor
    V[:, 0] = dot(rc, rc, 0, 0, HIGHEST).reshape(NZ, part, r)
    co = jnp.zeros((own, r), F32)
    xown = XB[d]
    for piece in split3(rc)[::-1]:
        co = co + dot(xown, piece, 1, 0)
    V[:, 1] = co.reshape(NZ, part, r)

    def place_v(zz, v):
        VF[zz] = v

    over_tensor(V, V1, V2, lambda zz: VF.at[zz], place_v)

    tt = VF[:, 1].reshape(own, r)
    mm = jnp.zeros((r, n), F32)
    for piece in split3(tt)[::-1]:
        mm = mm + dot(piece, U[...], 0, 0)
    M[...] = mm.reshape(NX, NC, r // (NX * NC), n)
    m1, m2 = take_recv(NX), take_recv(NX)
    for o in (2, 1, 3, 0):
        e = mod(x + o, NX)
        send(M.at[e, 1 - c], MS.at[e], m1 + e, twin)
    for o in (2, 1, 3, 0):
        e = mod(x + o, NX)
        arrive(MS.at[e], m1 + e)
        MC[e] = M[e, c] + MS[e]
        if o:
            send(MC.at[e], MR.at[x], m2 + x, at_xc(e, c))
    MR[x] = MC[x]

    inverse_factor(VF[:, 0].reshape(r, r), WK)

    for o in (1, 3, 2):
        e = mod(x + o, NX)
        arrive(MR.at[e], m2 + e)
    v = MR[0]
    for j in range(1, NX):
        v = v + MR[j]
    MF[d] = v
    inv = WK[:, r:]
    basis[...] = dot(rc, inv, 1, 1, HIGHEST) * math.sqrt(features)
    over_dp(lambda e: MF.at[e])
    corange[...] = dot(inv, MF[...].reshape(r, n), 1, 0, HIGHEST) * factor

    assert count["s"] <= 220 and count["r"] <= 230, count
    for cp, when in pending:
        if when is None:
            cp.wait_send()
        else:
            pl.when(when)(cp.wait_send)


def shards(out_grad, down_weight, gate_pre, inputs, test_matrix):
    rows, depth = out_grad.shape
    n = down_weight.shape[0]
    own, width = inputs.shape
    r = test_matrix.shape[1]
    half = rows // 2
    part = r // NZ
    dp = NX * NC
    vm = pltpu.VMEM
    scratch = [
        vm((8 * NY * 2, half, depth), BF16),
        vm((n, depth), BF16),
        vm((own, n), BF16),
        vm((dp, own, width), BF16),
        vm((n, r), BF16),
        vm((own, n), F32),
        vm((8 * NY * 2, half, n), F32),
        vm((8, 3, half, n), F32),
        vm((NZ // NC, 2, half, n), F32),
        vm((NZ // NC, 2, half, n), F32),
        vm((8, half, n), BF16),
        vm((8, half, n), BF16),
        vm((8, 2, half, n), BF16),
        vm((2, NZ // NC, 2, half, n), BF16),
        vm((own, n), BF16),
        vm((width, dp * own), BF16),
        vm((NZ, part, r), F32),
        vm((NZ, part, r), F32),
        vm((NY, part, r), F32),
        vm((dp, NZ, part, r), F32),
        vm((NZ, 2, part, r), F32),
        vm((NZ, 2, part, r), F32),
        vm((NY, 2, part, r), F32),
        vm((NZ, 2, part, r), F32),
        vm((r, 2 * r), F32),
        vm((NX, NC, r // dp, n), F32),
        vm((NX, r // dp, n), F32),
        vm((NX, r // dp, n), F32),
        vm((NX, r // dp, n), F32),
        vm((dp, r // dp, n), F32),
        pltpu.SemaphoreType.DMA((220,)),
        pltpu.SemaphoreType.DMA((230,)),
        pltpu.SemaphoreType.DMA((6,)),
    ]
    flops = 2 * dp * own * n * depth
    return pl.pallas_call(
        kernel,
        out_shape=(
            jax.ShapeDtypeStruct((width, r), F32),
            jax.ShapeDtypeStruct((r, n), F32),
        ),
        in_specs=[pl.BlockSpec(memory_space=pl.ANY)] * 5,
        out_specs=[pl.BlockSpec(memory_space=pltpu.VMEM)] * 2,
        scratch_shapes=scratch,
        cost_estimate=pl.CostEstimate(
            flops=flops, bytes_accessed=2 * n * depth, transcendentals=own * n
        ),
        compiler_params=pltpu.CompilerParams(
            collective_id=0, has_side_effects=True, vmem_limit_bytes=60 * 1024 * 1024
        ),
    )(out_grad, down_weight, gate_pre, inputs, test_matrix)


def solution(mesh):
    return jax.shard_map(
        shards,
        mesh=mesh,
        in_specs=(
            P("tensor", "dp"),
            P("tensor", "dp"),
            P("dp", "tensor"),
            P("dp", "tensor"),
            P("tensor", None),
        ),
        out_specs=(P("tensor", None), P(None, "tensor")),
        check_vma=False,
    )
```

```python
import functools
import math

import jax
import jax.numpy as jnp
from jax import lax
from jax.experimental import pallas as pl
from jax.experimental.pallas import tpu as pltpu
from jax.sharding import PartitionSpec as P

MESH = pl.DeviceIdType.MESH
F32 = jnp.float32
BF16 = jnp.bfloat16

NX, NC, NY, NZ = 4, 2, 4, 8
CUT = 1024
LAST = 2 * (NZ // 2) - 1


def slot_from_below(k):
    return LAST if k == NZ // 2 else 2 * k


def slot_from_above(k):
    return LAST if k == NZ // 2 else 2 * k - 1


OFFSET = {0: 0, LAST: NZ // 2}
STEP = {0: 0, LAST: NZ // 2}
for _k in range(1, NZ // 2):
    OFFSET[slot_from_below(_k)] = NZ - _k
    OFFSET[slot_from_above(_k)] = _k
    STEP[slot_from_below(_k)] = STEP[slot_from_above(_k)] = _k

ARRIVALS = [
        (2, 0, 0), (1, 0, 0), (0, 3, 1), (0, 1, 1), (2, 0, 1), (1, 0, 1), (0, 3, 0),
        (0, 1, 0), (0, 2, 1), (4, 0, 0), (3, 0, 0), (2, 3, 0), (2, 1, 0), (2, 3, 1),
        (1, 3, 1), (1, 3, 0), (1, 1, 0), (2, 1, 1), (1, 1, 1), (0, 2, 0), (4, 1, 0),
        (4, 0, 1), (3, 0, 1), (4, 3, 0), (3, 1, 0), (2, 2, 1), (1, 2, 1), (3, 3, 0),
        (1, 2, 0), (6, 0, 0), (5, 0, 0), (2, 2, 0), (4, 3, 1), (3, 3, 1), (4, 2, 0),
        (3, 2, 0), (4, 1, 1), (3, 1, 1), (6, 3, 0), (6, 1, 0), (6, 0, 1), (5, 0, 1),
        (5, 3, 0), (5, 1, 0), (4, 2, 1), (3, 2, 1), (7, 0, 0), (5, 3, 1), (6, 2, 0),
        (6, 3, 1), (5, 1, 1), (5, 2, 0), (6, 1, 1), (5, 2, 1), (7, 3, 0), (7, 1, 0),
        (7, 0, 1), (7, 3, 1), (6, 2, 1), (7, 2, 1), (7, 1, 1), (7, 2, 0),
]
HALF_TURN = {0: True, 1: True, 3: False, 2: False}


def split3(v):
    hi = v.astype(BF16)
    rest = v - hi.astype(F32)
    mid = rest.astype(BF16)
    low = (rest - mid.astype(F32)).astype(BF16)
    return hi, mid, low


def dot(a, b, ca, cb, precision=None):
    return lax.dot_general(
        a, b, (((ca,), (cb,)), ((), ())), preferred_element_type=F32, precision=precision
    )


HIGHEST = lax.Precision.HIGHEST


def inverse_factor(gram, work, midway):
    n = gram.shape[0]
    ri = lax.broadcasted_iota(jnp.int32, (n, n), 0)
    ci = lax.broadcasted_iota(jnp.int32, (n, n), 1)
    work[:, :n] = gram
    work[:, n:] = jnp.where(ri == ci, 1.0, 0.0).astype(F32)
    sub = lax.broadcasted_iota(jnp.int32, (8, n), 0)
    sub2 = lax.broadcasted_iota(jnp.int32, (8, 2 * n), 0)
    for b in range(n // 8):
        if b == n // 16:
            midway()
        rows = slice(8 * b, 8 * b + 8)
        panel = work[rows, :]
        cols = [
            jnp.broadcast_to(panel[:, 8 * b + m : 8 * b + m + 1], (8, n)) for m in range(8)
        ]
        for k in range(8):
            inv = lax.rsqrt(cols[k][k : k + 1, :])
            fac = jnp.where(sub > k, cols[k] * inv, 0.0)
            fac2 = jnp.concatenate([fac, fac], axis=1)
            inv2 = jnp.concatenate([inv, inv], axis=1)
            row = panel[k : k + 1, :] * inv2
            panel = jnp.where(sub2 == k, row, panel - fac2 * row)
            for m in range(k + 1, 8):
                cols[m] = cols[m] - fac * (cols[m][k : k + 1, :] * inv)
        work[rows, :] = panel
        done = 8 * (b + 1)
        if done < n:
            hi = panel.astype(BF16).astype(F32)
            mid = (panel - hi).astype(BF16).astype(F32)
            low = panel - hi - mid
            left = jnp.concatenate([hi, hi, mid, hi, low, mid], axis=0)[:, :n].astype(BF16)
            right = jnp.concatenate([hi, mid, hi, low, hi, mid], axis=0).astype(BF16)
            work[done:, :] = work[done:, :] - dot(left, right, 0, 0)[done:, :]


def kernel(
    og, dw, gate, inp, test, basis, corange,
    GA, GB, W, GT, XB, TM, SIL, PT, SIBR, SIB0, HG, XS, RX, UF, XT,
    SP, S1, S2, SF, RC, V, V1, V2, GF, TF, WK,
    sends, recvs, local,
):
    d, t = lax.axis_index("dp"), lax.axis_index("tensor")
    x, c = d // NC, lax.rem(d, NC)
    y, z = t // NZ, lax.rem(t, NZ)
    tokens = NX * NC * XB.shape[1]
    factor = 1.0 / math.sqrt(tokens)
    features = inp.shape[1] * NY * NZ

    def mod(a, n):
        return lax.rem(a + n, n)

    def at_yz(yy, zz):
        return {"dp": d, "tensor": yy * NZ + zz}

    def at_xc(xx, cc):
        return {"dp": xx * NC + cc, "tensor": t}

    def around(o, p):
        return {"dp": mod(x + o, NX) * NC + c, "tensor": y * NZ + mod(z + p, NZ)}

    zu, zd = at_yz(y, mod(z + 1, NZ)), at_yz(y, mod(z - 1, NZ))
    yu, yd, y2 = at_yz(mod(y + 1, NY), z), at_yz(mod(y - 1, NY), z), at_yz(mod(y + 2, NY), z)
    xu, xd = mod(x + 1, NX), mod(x - 1, NX)
    twin = at_xc(x, 1 - c)

    pending = []
    count = {"s": 0, "r": 0}

    def finish():
        assert count["s"] <= 280 and count["r"] <= 280, count
        for make, when in pending:
            if when is None:
                make().wait_send()
            else:
                pl.when(when)(make().wait_send)

    def take_recv(n):
        base = count["r"]
        count["r"] += n
        return base

    def send(src, dst, recv, dev, when=None):
        idx = count["s"]
        count["s"] += 1

        def make():
            return pltpu.make_async_remote_copy(
                src_ref=src() if callable(src) else src,
                dst_ref=dst() if callable(dst) else dst,
                send_sem=sends.at[idx], recv_sem=recvs.at[recv() if callable(recv) else recv],
                device_id=dev, device_id_type=MESH,
            )

        if when is None:
            make().start()
        else:
            pl.when(when)(make().start)
        pending.append((make, when))

    def arrive(ref, recv):
        pltpu.make_async_remote_copy(
            src_ref=ref, dst_ref=ref, send_sem=sends.at[0], recv_sem=recvs.at[recv],
            device_id=twin, device_id_type=MESH,
        ).wait_recv()

    q0, qp, qn, q2 = mod(y - x, NY), mod(y - 1 - x, NY), mod(y + 1 - x, NY), mod(y + 2 - x, NY)

    half = og.shape[0] // 2
    loads = [
        pltpu.make_async_copy(og.at[:, pl.ds(0, CUT)], GA.at[q0], local.at[0]),
        pltpu.make_async_copy(
            og.at[:, pl.ds(CUT, og.shape[1] - CUT)], GB.at[q0], local.at[5]
        ),
        pltpu.make_async_copy(inp, XB.at[d], local.at[1]),
        pltpu.make_async_copy(gate, GT, local.at[3]),
        pltpu.make_async_copy(dw, W, local.at[2]),
        pltpu.make_async_copy(test, TM, local.at[4]),
    ]
    for cp in loads:
        cp.start()

    barrier = pltpu.get_barrier_semaphore()
    peers = [zu, zd, yu, yd, y2] + [around(o, 0) for o in range(1, NX)] + [twin]
    for dev in peers:
        pl.semaphore_signal(barrier, inc=1, device_id=dev, device_id_type=MESH)
    pl.semaphore_wait(barrier, len(peers))
    loads[0].wait()
    loads[1].wait()

    ag = take_recv(8 * NY * 2)

    def item(slot, q, h):
        return (GB if h else GA).at[slot * NY + q]

    def mark(slot, q, h):
        return ag + (slot * NY + q) * 2 + h

    def pass_on(slot, q, h, to_slot, dev):
        send(
            lambda: item(slot, q, h), lambda: item(to_slot, q, h),
            lambda: mark(to_slot, q, h), dev
        )

    def got(slot, q, h):
        arrive(item(slot, q, h), mark(slot, q, h))

    below, above = slot_from_below, slot_from_above
    TOP = NZ // 2

    pass_on(0, q0, 0, below(1), zu)
    pass_on(0, q0, 0, above(1), zd)
    pass_on(0, q0, 1, 0, yu)
    pass_on(0, q0, 1, 0, yd)
    pass_on(0, q0, 1, below(1), zu)
    pass_on(0, q0, 1, above(1), zd)
    pass_on(0, q0, 0, 0, yu)
    pass_on(0, q0, 0, 0, yd)
    pass_on(0, q0, 1, 0, y2)

    loads[2].wait()
    xr = take_recv(NX * NC)
    for o in (1, 3, 2):
        send(XB.at[d], XB.at[d], xr + d, at_xc(mod(x + o, NX), c))
    send(XB.at[d], XB.at[d], xr + d, twin)

    row = [q0, qn, q2, qp]

    def arrival(slot, b, h):
        q, k, up = row[b], STEP[slot], slot % 2 == 0
        got(slot, q, h)
        if h:
            if slot == 0:
                pass_on(0, q, 1, below(1), zu)
                pass_on(0, q, 1, above(1), zd)
            elif slot != LAST and (k + 1 < TOP or HALF_TURN[b] == up):
                if up:
                    pass_on(slot, q, 1, below(k + 1), zu)
                else:
                    pass_on(slot, q, 1, above(k + 1), zd)
        elif b == 0:
            if slot != LAST:
                if up:
                    pass_on(slot, q, 0, below(k + 1), zu)
                elif k + 1 < TOP:
                    pass_on(slot, q, 0, above(k + 1), zd)
            pass_on(slot, q, 0, slot, yu)
            pass_on(slot, q, 0, slot, yd)
        elif b == 3 and up:
            pass_on(slot, q, 0, slot, yu)
        elif b == 1 and not up:
            pass_on(slot, q, 0, slot, yd)

    sibs = take_recv(NZ)
    sib0 = take_recv(NZ // NC * 2)
    rx = take_recv(3 * (NZ // NC) * 2)
    n = W.shape[0]
    WIDE = 256

    def column(s):
        return lax.rem(z + OFFSET[s], NZ)

    def owner_of(s):
        return column(s) // (NZ // NC), lax.rem(column(s), NZ // NC)

    def product(s0, slots, events):
        rows = slots * NY * 2 * half

        def cols_at(start, width):
            blocks = pl.ds(s0 * NY, slots * NY)
            a = jnp.concatenate(
                [g[blocks].reshape(rows, g.shape[2]) for g in (GA, GB)], axis=1
            )
            b = W[pl.ds(start, width), :]
            v = dot(a, b, 1, 1).reshape(slots, NY, 2, half, width)
            for h in range(2):
                PT[pl.ds(s0, slots), h, :, :, pl.ds(start, width)] = v[:, :, h]

        def body(j, _):
            cols_at(pl.multiple_of(j * WIDE, WIDE), WIDE)
            for i, todo in enumerate(events):
                if todo:

                    @pl.when(j == i)
                    def _():
                        for act in todo:
                            act()

            return 0

        assert len(events) <= n // WIDE
        lax.fori_loop(0, n // WIDE, body, 0)
        if n % WIDE:
            cols_at(n - n % WIDE, n % WIDE)

    def exchange(s):
        core, zc = owner_of(s)
        send(
            lambda: PT.at[s, 1 - c, pl.ds(1, NX - 1)], lambda: SIBR.at[s], sibs + s, twin
        )
        for h in range(2):
            send(
                lambda h=h: PT.at[s, h, 0], lambda h=h: SIB0.at[zc, h], sib0 + zc * 2 + h,
                twin, core != c,
            )

        @pl.when(core == c)
        def _():
            HG[zc] = PT[s, :, 0]

    owners = [owner_of(s) for s in range(NZ)]
    targets = [[at_xc(mod(x + o, NX), owners[s][0]) for o in range(1, NX)] for s in range(NZ)]
    marks = [
        [rx + ((o - 1) * (NZ // NC) + owners[s][1]) * 2 + c for o in range(1, NX)]
        for s in range(NZ)
    ]

    def outward(s):
        zc = owners[s][1]
        arrive(SIBR.at[s], sibs + s)
        XS[s] = (PT[s, c, 1:] + SIBR[s]).astype(BF16)
        for o in (2, 1, 3):
            send(
                lambda o=o: XS.at[s, o - 1], lambda o=o: RX.at[o - 1, zc, c],
                marks[s][o - 1], targets[s][o - 1],
            )

    def own(s):
        core, zc = owners[s]

        @pl.when(core == c)
        def _():
            for h in range(2):
                arrive(SIB0.at[zc, h], sib0 + zc * 2 + h)
            v = HG[zc] + SIB0[zc]
            for o in range(1, NX):
                for h in range(2):
                    arrive(
                        RX.at[o - 1, zc, h], rx + ((o - 1) * (NZ // NC) + zc) * 2 + h
                    )
                v = v + RX[o - 1, zc].astype(F32)
            UF[d, zc] = (v * SIL[zc].reshape(2, half, n)).astype(BF16)

    groups = [[0]] + [[above(k), below(k)] for k in range(1, TOP)] + [[LAST]]
    ends = [
        1 + max(i for i, a in enumerate(ARRIVALS) if a[0] in g) for g in groups
    ]

    def to_other_core():
        for o in (1, 3, 2):
            e = mod(x + o, NX) * NC + c
            arrive(XB.at[e], xr + e)
            send(XB.at[e], XB.at[e], xr + e, twin)

    def transposed():
        rows = XB.shape[1]
        for o in range(NX):
            e = mod(x + o, NX) * NC + 1 - c
            arrive(XB.at[e], xr + e)
        for e in range(NX * NC):
            XT[:, e * rows : (e + 1) * rows] = XB[e].T

    loads[3].wait()
    g = GT[...].astype(F32)
    SIL[...] = (g * (1.0 / (1.0 + jnp.exp(-g)))).reshape(SIL.shape)
    for a in ARRIVALS[: ends[0]]:
        arrival(*a)
    loads[4].wait()
    turns = n // WIDE
    for k in range(TOP + 1):
        todo = ARRIVALS[ends[k] : ends[k + 1]] if k < TOP else []
        each = max(2, -(-len(todo) // turns))
        events = [
            [functools.partial(arrival, *a) for a in todo[i * each : (i + 1) * each]]
            for i in range(turns)
        ]
        if k >= 1:
            events[3] += [functools.partial(outward, s) for s in groups[k - 1]]
        if k >= 2:
            events[5] += [functools.partial(own, s) for s in groups[k - 2]]
        product(groups[k][0], len(groups[k]), events)
        for s in groups[k]:
            exchange(s)
        if k == 1:
            to_other_core()
        if k == 2:
            transposed()
    outward(LAST)
    loads[5].wait()
    for s in groups[TOP - 1] + groups[TOP]:
        own(s)
    ur = take_recv(NX * NC * 2)
    most = NZ // NC - 1

    def rows_to(o, first, count, k):
        block = UF.at[d, pl.ds(first, count)]
        send(block, block, ur + d * 2 + k, at_xc(mod(x + o, NX), c))

    def up_grad_to_twin():
        for o in (1, 3, 2):
            e = mod(x + o, NX) * NC + c
            if o == 2:
                arrive(UF.at[e], ur + e * 2)
            else:
                arrive(UF.at[e, pl.ds(0, most)], ur + e * 2)
                arrive(UF.at[e, pl.ds(most, 1)], ur + e * 2 + 1)
            send(UF.at[e], UF.at[e], ur + e * 2, twin)

    def up_grad_from_twin():
        for o in range(NX):
            e = mod(x + o, NX) * NC + 1 - c
            arrive(UF.at[e], ur + e * 2)

    rows_to(1, 0, most, 0)
    rows_to(3, 0, most, 0)
    send(UF.at[d], UF.at[d], ur + d * 2, twin)

    r = TM.shape[1]
    part = r // NZ
    rows_own = XB.shape[1]

    def summed(src, first, second):
        r1, r2 = take_recv(NZ), take_recv(NY)
        first[z] = src[z]
        for o in (4, 3, 5, 2, 6, 1, 7):
            zz = mod(z + o, NZ)
            send(src.at[zz], first.at[z], r1 + z, at_yz(y, zz))
        for o in (1, 7, 2, 6, 3, 5, 4):
            zz = mod(z + o, NZ)
            arrive(first.at[zz], r1 + zz)
        v = first[0]
        for j in range(1, NZ):
            v = v + first[j]
        second[y] = v
        for o in (2, 1, 3):
            send(second.at[y], second.at[y], r2 + y, at_yz(mod(y + o, NY), z))
        for o in (1, 3, 2):
            yy = mod(y + o, NY)
            arrive(second.at[yy], r2 + yy)
        v = second[0]
        for j in range(1, NY):
            v = v + second[j]
        return v

    pairs = [(o, p) for o in (2, 1, 3, 0) for p in (4, 3, 5, 2, 6, 1, 7, 0) if o or p]

    def spread(full):
        base = take_recv(NX * NZ)
        for o, p in pairs:
            send(full.at[d, z], full.at[d, z], base + x * NZ + z, around(o, p))
        return base

    def collect(full, base):
        other = take_recv(NX)
        for o in (0, 1, 3, 2):
            xx = mod(x + o, NX)
            for p in (0, 1, 7, 2, 6, 3, 5, 4):
                if o or p:
                    zz = mod(z + p, NZ)
                    arrive(full.at[xx * NC + c, zz], base + xx * NZ + zz)
            send(full.at[xx * NC + c], full.at[xx * NC + c], other + xx, twin)
        return other

    def from_twin(full, other):
        for o in (0, 1, 3, 2):
            xx = mod(x + o, NX)
            arrive(full.at[xx * NC + 1 - c], other + xx)

    u = UF[d].reshape(rows_own, n)
    SP[...] = dot(u, TM[...], 1, 0).reshape(NZ, part, r)
    v = summed(SP, S1, S2)
    SF[d, z] = v
    base = spread(SF)
    rows_to(1, most, 1, 1)
    rows_to(3, most, 1, 1)
    rows_to(2, 0, most + 1, 0)
    other = collect(SF, base)
    from_twin(SF, other)

    s = SF[...].reshape(tokens, r)
    rc = jnp.zeros((XT.shape[0], r), F32)
    xt = XT[...]
    for piece in split3(s)[::-1]:
        rc = rc + dot(xt, piece, 1, 0)
    rc = rc * factor
    RC[...] = rc
    V[:, 0] = dot(rc, rc, 0, 0, HIGHEST).reshape(NZ, part, r)
    co = jnp.zeros((rows_own, r), F32)
    xown = XB[d]
    for piece in split3(rc)[::-1]:
        co = co + dot(xown, piece, 1, 0)
    V[:, 1] = co.reshape(NZ, part, r)
    v = summed(V, V1, V2)
    GF[z] = v[0]
    TF[d, z] = v[1]
    gr = take_recv(NZ)
    for o in (4, 3, 5, 2, 6, 1, 7):
        send(GF.at[z], GF.at[z], gr + z, at_yz(y, mod(z + o, NZ)))
    base = spread(TF)

    up_grad_to_twin()
    for o in (1, 7, 2, 6, 3, 5, 4):
        zz = mod(z + o, NZ)
        arrive(GF.at[zz], gr + zz)

    others = []
    inverse_factor(
        GF[...].reshape(r, r), WK, lambda: others.append(collect(TF, base))
    )
    inv = WK[:, r:]
    basis[...] = dot(RC[...], inv, 1, 1, HIGHEST) * math.sqrt(features)
    from_twin(TF, others[0])
    up_grad_from_twin()
    cot = dot(inv, TF[...].reshape(tokens, r), 1, 1, HIGHEST) * factor
    hi = cot.astype(BF16)
    low = (cot - hi.astype(F32)).astype(BF16)
    both = dot(jnp.concatenate([hi, low], axis=0), UF[...].reshape(tokens, n), 1, 0)
    corange[...] = both[:r] + both[r:]
    finish()


def shards(out_grad, down_weight, gate_pre, inputs, test_matrix):
    rows, depth = out_grad.shape
    n = down_weight.shape[0]
    own, width = inputs.shape
    r = test_matrix.shape[1]
    half = rows // 2
    part = r // NZ
    dp = NX * NC
    vm = pltpu.VMEM
    scratch = [
        vm((NZ * NY, rows, CUT), BF16),
        vm((NZ * NY, rows, depth - CUT), BF16),
        vm((n, depth), BF16),
        vm((own, n), BF16),
        vm((dp, own, width), BF16),
        vm((n, r), BF16),
        vm((NZ // NC, rows, n), F32),
        vm((NZ, 2, NY, half, n), F32),
        vm((NZ, NX - 1, half, n), F32),
        vm((NZ // NC, 2, half, n), F32),
        vm((NZ // NC, 2, half, n), F32),
        vm((NZ, NX - 1, half, n), BF16),
        vm((NX - 1, NZ // NC, 2, half, n), BF16),
        vm((dp, NZ // NC, 2, half, n), BF16),
        vm((width, dp * own), BF16),
        vm((NZ, part, r), F32),
        vm((NZ, part, r), F32),
        vm((NY, part, r), F32),
        vm((dp, NZ, part, r), F32),
        vm((width, r), F32),
        vm((NZ, 2, part, r), F32),
        vm((NZ, 2, part, r), F32),
        vm((NY, 2, part, r), F32),
        vm((NZ, part, r), F32),
        vm((dp, NZ, part, r), F32),
        vm((r, 2 * r), F32),
        pltpu.SemaphoreType.DMA((280,)),
        pltpu.SemaphoreType.DMA((280,)),
        pltpu.SemaphoreType.DMA((6,)),
    ]
    flops = 2 * dp * own * n * depth
    return pl.pallas_call(
        kernel,
        out_shape=(
            jax.ShapeDtypeStruct((width, r), F32),
            jax.ShapeDtypeStruct((r, n), F32),
        ),
        in_specs=[pl.BlockSpec(memory_space=pl.ANY)] * 5,
        out_specs=[pl.BlockSpec(memory_space=pltpu.VMEM)] * 2,
        scratch_shapes=scratch,
        cost_estimate=pl.CostEstimate(
            flops=flops, bytes_accessed=2 * n * depth, transcendentals=own * n
        ),
        compiler_params=pltpu.CompilerParams(
            collective_id=0, has_side_effects=True, vmem_limit_bytes=60 * 1024 * 1024
        ),
    )(out_grad, down_weight, gate_pre, inputs, test_matrix)


def solution(mesh):
    return jax.shard_map(
        shards,
        mesh=mesh,
        in_specs=(
            P("tensor", "dp"),
            P("tensor", "dp"),
            P("dp", "tensor"),
            P("dp", "tensor"),
            P("tensor", None),
        ),
        out_specs=(P("tensor", None), P(None, "tensor")),
        check_vma=False,
    )
```

```python
import functools
import math

import jax
import jax.numpy as jnp
from jax import lax
from jax.experimental import pallas as pl
from jax.experimental.pallas import tpu as pltpu
from jax.sharding import PartitionSpec as P

MESH = pl.DeviceIdType.MESH
F32 = jnp.float32
BF16 = jnp.bfloat16

NX, NC, NY, NZ = 4, 2, 4, 8
CUT = 1024
LAST = 2 * (NZ // 2) - 1


def slot_from_below(k):
    return LAST if k == NZ // 2 else 2 * k


def slot_from_above(k):
    return LAST if k == NZ // 2 else 2 * k - 1


OFFSET = {0: 0, LAST: NZ // 2}
STEP = {0: 0, LAST: NZ // 2}
for _k in range(1, NZ // 2):
    OFFSET[slot_from_below(_k)] = NZ - _k
    OFFSET[slot_from_above(_k)] = _k
    STEP[slot_from_below(_k)] = STEP[slot_from_above(_k)] = _k

ARRIVALS = [
        (2, 0, 0), (1, 0, 0), (0, 3, 1), (0, 1, 1), (2, 0, 1), (1, 0, 1), (0, 3, 0),
        (0, 1, 0), (0, 2, 1), (4, 0, 0), (3, 0, 0), (2, 3, 0), (2, 1, 0), (2, 3, 1),
        (1, 3, 1), (1, 3, 0), (1, 1, 0), (2, 1, 1), (1, 1, 1), (0, 2, 0), (4, 1, 0),
        (4, 0, 1), (3, 0, 1), (4, 3, 0), (3, 1, 0), (2, 2, 1), (1, 2, 1), (3, 3, 0),
        (1, 2, 0), (6, 0, 0), (5, 0, 0), (2, 2, 0), (4, 3, 1), (3, 3, 1), (4, 2, 0),
        (3, 2, 0), (4, 1, 1), (3, 1, 1), (6, 3, 0), (6, 1, 0), (6, 0, 1), (5, 0, 1),
        (5, 3, 0), (5, 1, 0), (4, 2, 1), (3, 2, 1), (7, 0, 0), (5, 3, 1), (6, 2, 0),
        (6, 3, 1), (5, 1, 1), (5, 2, 0), (6, 1, 1), (5, 2, 1), (7, 3, 0), (7, 1, 0),
        (7, 0, 1), (7, 3, 1), (6, 2, 1), (7, 2, 1), (7, 1, 1), (7, 2, 0),
]
HALF_TURN = {0: True, 1: True, 3: False, 2: False}


def split3(v):
    hi = v.astype(BF16)
    rest = v - hi.astype(F32)
    mid = rest.astype(BF16)
    low = (rest - mid.astype(F32)).astype(BF16)
    return hi, mid, low


def dot(a, b, ca, cb, precision=None):
    return lax.dot_general(
        a, b, (((ca,), (cb,)), ((), ())), preferred_element_type=F32, precision=precision
    )


HIGHEST = lax.Precision.HIGHEST


def inverse_factor(gram, work):
    n = gram.shape[0]
    ri = lax.broadcasted_iota(jnp.int32, (n, n), 0)
    ci = lax.broadcasted_iota(jnp.int32, (n, n), 1)
    work[:, :n] = gram
    work[:, n:] = jnp.where(ri == ci, 1.0, 0.0).astype(F32)
    sub = lax.broadcasted_iota(jnp.int32, (8, n), 0)
    sub2 = lax.broadcasted_iota(jnp.int32, (8, 2 * n), 0)
    for b in range(n // 8):
        rows = slice(8 * b, 8 * b + 8)
        panel = work[rows, :]
        cols = [
            jnp.broadcast_to(panel[:, 8 * b + m : 8 * b + m + 1], (8, n)) for m in range(8)
        ]
        for k in range(8):
            inv = lax.rsqrt(cols[k][k : k + 1, :])
            fac = jnp.where(sub > k, cols[k] * inv, 0.0)
            fac2 = jnp.concatenate([fac, fac], axis=1)
            inv2 = jnp.concatenate([inv, inv], axis=1)
            row = panel[k : k + 1, :] * inv2
            panel = jnp.where(sub2 == k, row, panel - fac2 * row)
            for m in range(k + 1, 8):
                cols[m] = cols[m] - fac * (cols[m][k : k + 1, :] * inv)
        work[rows, :] = panel
        done = 8 * (b + 1)
        if done < n:
            hi = panel.astype(BF16).astype(F32)
            mid = (panel - hi).astype(BF16).astype(F32)
            low = panel - hi - mid
            left = jnp.concatenate([hi, hi, mid, hi, low, mid], axis=0)[:, :n].astype(BF16)
            right = jnp.concatenate([hi, mid, hi, low, hi, mid], axis=0).astype(BF16)
            work[done:, :] = work[done:, :] - dot(left, right, 0, 0)[done:, :]


def kernel(
    og, dw, gate, inp, test, basis, corange,
    GA, GB, W, GT, XB, TM, SIL, PT, SIBR, SIB0, HG, XS, RX, UF,
    SP, S1, S2, SF, RC, KP, KR, KY, TF, WK,
    sends, recvs, local,
):
    d, t = lax.axis_index("dp"), lax.axis_index("tensor")
    x, c = d // NC, lax.rem(d, NC)
    y, z = t // NZ, lax.rem(t, NZ)
    tokens = NX * NC * XB.shape[1]
    factor = 1.0 / math.sqrt(tokens)
    features = inp.shape[1] * NY * NZ

    def mod(a, n):
        return lax.rem(a + n, n)

    def at_yz(yy, zz):
        return {"dp": d, "tensor": yy * NZ + zz}

    def at_xc(xx, cc):
        return {"dp": xx * NC + cc, "tensor": t}

    def around(o, p):
        return {"dp": mod(x + o, NX) * NC + c, "tensor": y * NZ + mod(z + p, NZ)}

    zu, zd = at_yz(y, mod(z + 1, NZ)), at_yz(y, mod(z - 1, NZ))
    yu, yd, y2 = at_yz(mod(y + 1, NY), z), at_yz(mod(y - 1, NY), z), at_yz(mod(y + 2, NY), z)
    xu, xd = mod(x + 1, NX), mod(x - 1, NX)
    twin = at_xc(x, 1 - c)

    pending = []
    count = {"s": 0, "r": 0}

    def finish():
        assert count["s"] <= 340 and count["r"] <= 340, count
        for make, when in pending:
            if when is None:
                make().wait_send()
            else:
                pl.when(when)(make().wait_send)

    def take_recv(n):
        base = count["r"]
        count["r"] += n
        return base

    def send(src, dst, recv, dev, when=None):
        idx = count["s"]
        count["s"] += 1

        def make():
            return pltpu.make_async_remote_copy(
                src_ref=src() if callable(src) else src,
                dst_ref=dst() if callable(dst) else dst,
                send_sem=sends.at[idx], recv_sem=recvs.at[recv() if callable(recv) else recv],
                device_id=dev, device_id_type=MESH,
            )

        if when is None:
            make().start()
        else:
            pl.when(when)(make().start)
        pending.append((make, when))

    def arrive(ref, recv):
        pltpu.make_async_remote_copy(
            src_ref=ref, dst_ref=ref, send_sem=sends.at[0], recv_sem=recvs.at[recv],
            device_id=twin, device_id_type=MESH,
        ).wait_recv()

    q0, qp, qn, q2 = mod(y - x, NY), mod(y - 1 - x, NY), mod(y + 1 - x, NY), mod(y + 2 - x, NY)

    half = og.shape[0] // 2
    loads = [
        pltpu.make_async_copy(og.at[:, pl.ds(0, CUT)], GA.at[q0], local.at[0]),
        pltpu.make_async_copy(
            og.at[:, pl.ds(CUT, og.shape[1] - CUT)], GB.at[q0], local.at[5]
        ),
        pltpu.make_async_copy(inp, XB.at[d], local.at[1]),
        pltpu.make_async_copy(gate, GT, local.at[3]),
        pltpu.make_async_copy(dw, W, local.at[2]),
        pltpu.make_async_copy(test, TM, local.at[4]),
    ]
    for cp in loads:
        cp.start()

    barrier = pltpu.get_barrier_semaphore()
    peers = [zu, zd, yu, yd, y2] + [around(o, 0) for o in range(1, NX)] + [twin]
    for dev in peers:
        pl.semaphore_signal(barrier, inc=1, device_id=dev, device_id_type=MESH)
    pl.semaphore_wait(barrier, len(peers))
    loads[0].wait()
    loads[1].wait()

    ag = take_recv(8 * NY * 2)

    def item(slot, q, h):
        return (GB if h else GA).at[slot * NY + q]

    def mark(slot, q, h):
        return ag + (slot * NY + q) * 2 + h

    def pass_on(slot, q, h, to_slot, dev):
        send(
            lambda: item(slot, q, h), lambda: item(to_slot, q, h),
            lambda: mark(to_slot, q, h), dev
        )

    def got(slot, q, h):
        arrive(item(slot, q, h), mark(slot, q, h))

    below, above = slot_from_below, slot_from_above
    TOP = NZ // 2

    pass_on(0, q0, 0, below(1), zu)
    pass_on(0, q0, 0, above(1), zd)
    pass_on(0, q0, 1, 0, yu)
    pass_on(0, q0, 1, 0, yd)
    pass_on(0, q0, 1, below(1), zu)
    pass_on(0, q0, 1, above(1), zd)
    pass_on(0, q0, 0, 0, yu)
    pass_on(0, q0, 0, 0, yd)
    pass_on(0, q0, 1, 0, y2)

    loads[2].wait()
    xr = take_recv(NX * NC)
    for o in (1, 3, 2):
        send(XB.at[d], XB.at[d], xr + d, at_xc(mod(x + o, NX), c))
    send(XB.at[d], XB.at[d], xr + d, twin)

    row = [q0, qn, q2, qp]

    def arrival(slot, b, h):
        q, k, up = row[b], STEP[slot], slot % 2 == 0
        got(slot, q, h)
        if h:
            if slot == 0:
                pass_on(0, q, 1, below(1), zu)
                pass_on(0, q, 1, above(1), zd)
            elif slot != LAST and (k + 1 < TOP or HALF_TURN[b] == up):
                if up:
                    pass_on(slot, q, 1, below(k + 1), zu)
                else:
                    pass_on(slot, q, 1, above(k + 1), zd)
        elif b == 0:
            if slot != LAST:
                if up:
                    pass_on(slot, q, 0, below(k + 1), zu)
                elif k + 1 < TOP:
                    pass_on(slot, q, 0, above(k + 1), zd)
            pass_on(slot, q, 0, slot, yu)
            pass_on(slot, q, 0, slot, yd)
        elif b == 3 and up:
            pass_on(slot, q, 0, slot, yu)
        elif b == 1 and not up:
            pass_on(slot, q, 0, slot, yd)

    sibs = take_recv(NZ)
    sib0 = take_recv(NZ // NC * 2)
    rx = take_recv(3 * (NZ // NC) * 2)
    n = W.shape[0]
    WIDE = 256

    def column(s):
        return lax.rem(z + OFFSET[s], NZ)

    def owner_of(s):
        return column(s) // (NZ // NC), lax.rem(column(s), NZ // NC)

    def product(s0, slots, events):
        rows = slots * NY * 2 * half

        def cols_at(start, width):
            blocks = pl.ds(s0 * NY, slots * NY)
            a = jnp.concatenate(
                [g[blocks].reshape(rows, g.shape[2]) for g in (GA, GB)], axis=1
            )
            b = W[pl.ds(start, width), :]
            v = dot(a, b, 1, 1).reshape(slots, NY, 2, half, width)
            for h in range(2):
                PT[pl.ds(s0, slots), h, :, :, pl.ds(start, width)] = v[:, :, h]

        def body(j, _):
            cols_at(pl.multiple_of(j * WIDE, WIDE), WIDE)
            for i, todo in enumerate(events):
                if todo:

                    @pl.when(j == i)
                    def _():
                        for act in todo:
                            act()

            return 0

        assert len(events) <= n // WIDE
        lax.fori_loop(0, n // WIDE, body, 0)
        if n % WIDE:
            cols_at(n - n % WIDE, n % WIDE)

    def exchange(s):
        core, zc = owner_of(s)
        send(
            lambda: PT.at[s, 1 - c, pl.ds(1, NX - 1)], lambda: SIBR.at[s], sibs + s, twin
        )
        for h in range(2):
            send(
                lambda h=h: PT.at[s, h, 0], lambda h=h: SIB0.at[zc, h], sib0 + zc * 2 + h,
                twin, core != c,
            )

        @pl.when(core == c)
        def _():
            HG[zc] = PT[s, :, 0]

    owners = [owner_of(s) for s in range(NZ)]
    targets = [[at_xc(mod(x + o, NX), owners[s][0]) for o in range(1, NX)] for s in range(NZ)]
    marks = [
        [rx + ((o - 1) * (NZ // NC) + owners[s][1]) * 2 + c for o in range(1, NX)]
        for s in range(NZ)
    ]

    def outward(s):
        zc = owners[s][1]
        arrive(SIBR.at[s], sibs + s)
        XS[s] = (PT[s, c, 1:] + SIBR[s]).astype(BF16)
        for o in (2, 1, 3):
            send(
                lambda o=o: XS.at[s, o - 1], lambda o=o: RX.at[o - 1, zc, c],
                marks[s][o - 1], targets[s][o - 1],
            )

    def own(s):
        core, zc = owners[s]

        @pl.when(core == c)
        def _():
            for h in range(2):
                arrive(SIB0.at[zc, h], sib0 + zc * 2 + h)
            v = HG[zc] + SIB0[zc]
            for o in range(1, NX):
                for h in range(2):
                    arrive(
                        RX.at[o - 1, zc, h], rx + ((o - 1) * (NZ // NC) + zc) * 2 + h
                    )
                v = v + RX[o - 1, zc].astype(F32)
            UF[d, zc] = (v * SIL[zc].reshape(2, half, n)).astype(BF16)

    groups = [[0]] + [[above(k), below(k)] for k in range(1, TOP)] + [[LAST]]
    ur, tr = take_recv(NX * NC * (NZ // NC)), take_recv(NX * NC)
    same_core = [at_xc(mod(x + o, NX), c) for o in range(NX)]
    mine = [owners[s][0] == c for s in range(NZ)]
    row_marks = [ur + d * (NZ // NC) + owners[s][1] for s in range(NZ)]

    def rows_out(s):
        core, zc = owners[s]
        for o in (2, 1, 3):
            send(
                lambda: UF.at[d, zc], lambda: UF.at[d, zc], row_marks[s], same_core[o], mine[s]
            )

    ends = [
        1 + max(i for i, a in enumerate(ARRIVALS) if a[0] in g) for g in groups
    ]

    def to_other_core():
        for o in (1, 3, 2):
            e = mod(x + o, NX) * NC + c
            arrive(XB.at[e], xr + e)
            send(XB.at[e], XB.at[e], xr + e, twin)

    def inner_terms():
        rows, width = XB.shape[1], XB.shape[2]
        for o in range(NX):
            e = mod(x + o, NX) * NC + 1 - c
            arrive(XB.at[e], xr + e)
        v = dot(XB[d], XB[...].reshape(NX * NC * rows, width), 1, 1)
        part, wide = KP.shape[2], KP.shape[3]
        for zz in range(NZ):
            for yy in range(NY):
                KP[zz, yy] = v[
                    zz * part : (zz + 1) * part, yy * wide : (yy + 1) * wide
                ]

    kr, ky = take_recv(NY * NZ), take_recv(NY)
    hops = [(o, p) for p in (4, 3, 5, 2, 6, 1, 7, 0) for o in (2, 1, 3, 0) if o or p]

    def inner_out():
        for o, p in hops:
            yy, zz = mod(y + o, NY), mod(z + p, NZ)
            send(KP.at[zz, yy], KR.at[t], kr + t, at_yz(yy, zz))
        KR[t] = KP[z, y]

    def inner_sum():
        for o, p in hops[::-1]:
            tt = mod(y + o, NY) * NZ + mod(z + p, NZ)
            arrive(KR.at[tt], kr + tt)
        v = KR[0]
        for j in range(1, NY * NZ):
            v = v + KR[j]
        KY[y] = v
        for o in (2, 1, 3):
            send(KY.at[y], KY.at[y], ky + y, at_yz(mod(y + o, NY), z))

    def inner_rows():
        for o in (1, 3, 2):
            yy = mod(y + o, NY)
            arrive(KY.at[yy], ky + yy)
        return jnp.concatenate([KY[j] for j in range(NY)], axis=1)

    loads[3].wait()
    g = GT[...].astype(F32)
    SIL[...] = (g * (1.0 / (1.0 + jnp.exp(-g)))).reshape(SIL.shape)
    for a in ARRIVALS[: ends[0]]:
        arrival(*a)
    loads[4].wait()
    turns = n // WIDE
    for k in range(TOP + 1):
        todo = ARRIVALS[ends[k] : ends[k + 1]] if k < TOP else []
        each = max(2, -(-len(todo) // turns))
        events = [
            [functools.partial(arrival, *a) for a in todo[i * each : (i + 1) * each]]
            for i in range(turns)
        ]
        if k >= 1:
            events[3] += [functools.partial(outward, s) for s in groups[k - 1]]
        if k >= 2:
            for s in groups[k - 2]:
                events[5].append(functools.partial(own, s))
                if k < TOP:
                    events[5].append(functools.partial(rows_out, s))
        if k == TOP:
            inner_out()
        product(groups[k][0], len(groups[k]), events)
        for s in groups[k]:
            exchange(s)
        if k == 1:
            to_other_core()
        if k == 2:
            inner_terms()
    outward(LAST)
    loads[5].wait()
    for s in groups[TOP - 1] + groups[TOP]:
        own(s)
    for k in range(TOP - 2, TOP + 1):
        for s in groups[k]:
            rows_out(s)
    send(UF.at[d], UF.at[d], tr + d, twin)

    def up_grad_to_twin():
        for o in (1, 3, 2):
            e = mod(x + o, NX) * NC + c
            for zc in range(NZ // NC):
                arrive(UF.at[e, zc], ur + e * (NZ // NC) + zc)
            send(UF.at[e], UF.at[e], tr + e, twin)

    def up_grad_from_twin():
        for o in range(NX):
            e = mod(x + o, NX) * NC + 1 - c
            arrive(UF.at[e], tr + e)

    r = TM.shape[1]
    part = r // NZ
    rows_own = XB.shape[1]

    def summed(src, first, second, between):
        r1, r2 = take_recv(NZ), take_recv(NY)
        first[z] = src[z]
        for o in (4, 3, 5, 2, 6, 1, 7):
            zz = mod(z + o, NZ)
            send(src.at[zz], first.at[z], r1 + z, at_yz(y, zz))
        for o in (1, 7, 2, 6, 3, 5, 4):
            zz = mod(z + o, NZ)
            arrive(first.at[zz], r1 + zz)
        v = first[0]
        for j in range(1, NZ):
            v = v + first[j]
        second[y] = v
        for o in (2, 1, 3):
            send(second.at[y], second.at[y], r2 + y, at_yz(mod(y + o, NY), z))
        between()
        for o in (1, 3, 2):
            yy = mod(y + o, NY)
            arrive(second.at[yy], r2 + yy)
        v = second[0]
        for j in range(1, NY):
            v = v + second[j]
        return v

    pairs = [(o, p) for o in (2, 1, 3, 0) for p in (4, 3, 5, 2, 6, 1, 7, 0) if o or p]

    def spread(full):
        base = take_recv(NX * NZ)
        for o, p in pairs:
            send(full.at[d, z], full.at[d, z], base + x * NZ + z, around(o, p))
        return base

    def collect(full, base):
        other = take_recv(NX)
        for o in (0, 1, 3, 2):
            xx = mod(x + o, NX)
            for p in (0, 1, 7, 2, 6, 3, 5, 4):
                if o or p:
                    zz = mod(z + p, NZ)
                    arrive(full.at[xx * NC + c, zz], base + xx * NZ + zz)
            send(full.at[xx * NC + c], full.at[xx * NC + c], other + xx, twin)
        return other

    def from_twin(full, other):
        for o in (0, 1, 3, 2):
            xx = mod(x + o, NX)
            arrive(full.at[xx * NC + 1 - c], other + xx)

    u = UF[d].reshape(rows_own, n)
    SP[...] = dot(u, TM[...], 1, 0).reshape(NZ, part, r)
    v = summed(SP, S1, S2, inner_sum)
    SF[d, z] = v
    base = spread(SF)
    inner = inner_rows()
    other = collect(SF, base)
    from_twin(SF, other)

    s = SF[...].reshape(tokens, r)
    TF[d, z] = dot(inner, s, 1, 0, HIGHEST) * factor
    base = spread(TF)

    every = XB[...].reshape(tokens, XB.shape[2])
    rc = dot(every, jnp.concatenate(split3(s), axis=1), 0, 0)
    RC[...] = (rc[:, :r] + (rc[:, r : 2 * r] + rc[:, 2 * r :])) * factor
    up_grad_to_twin()
    from_twin(TF, collect(TF, base))
    tt = TF[...].reshape(tokens, r)
    inverse_factor(dot(SF[...].reshape(tokens, r), tt, 0, 0, HIGHEST) * factor, WK)
    inv = WK[:, r:]
    basis[...] = dot(RC[...], inv, 1, 1, HIGHEST) * math.sqrt(features)
    up_grad_from_twin()
    cot = dot(inv, tt, 1, 1, HIGHEST) * factor
    hi = cot.astype(BF16)
    low = (cot - hi.astype(F32)).astype(BF16)
    both = dot(jnp.concatenate([hi, low], axis=0), UF[...].reshape(tokens, n), 1, 0)
    corange[...] = both[:r] + both[r:]
    finish()


def hand_over(basis_in, corange_in, basis, corange, basis_held, corange_held, done):
    into = [
        pltpu.make_async_copy(basis_in, basis_held, done.at[0]),
        pltpu.make_async_copy(corange_in, corange_held, done.at[1]),
    ]
    out = [
        pltpu.make_async_copy(basis_held, basis, done.at[2]),
        pltpu.make_async_copy(corange_held, corange, done.at[3]),
    ]
    for cp in into:
        cp.start()
    for first, second in zip(into, out):
        first.wait()
        second.start()
    for cp in out:
        cp.wait()


def shards(out_grad, down_weight, gate_pre, inputs, test_matrix):
    rows, depth = out_grad.shape
    n = down_weight.shape[0]
    own, width = inputs.shape
    r = test_matrix.shape[1]
    half = rows // 2
    part = r // NZ
    dp = NX * NC
    vm = pltpu.VMEM
    scratch = [
        vm((NZ * NY, rows, CUT), BF16),
        vm((NZ * NY, rows, depth - CUT), BF16),
        vm((n, depth), BF16),
        vm((own, n), BF16),
        vm((dp, own, width), BF16),
        vm((n, r), BF16),
        vm((NZ // NC, rows, n), F32),
        vm((NZ, 2, NY, half, n), F32),
        vm((NZ, NX - 1, half, n), F32),
        vm((NZ // NC, 2, half, n), F32),
        vm((NZ // NC, 2, half, n), F32),
        vm((NZ, NX - 1, half, n), BF16),
        vm((NX - 1, NZ // NC, 2, half, n), BF16),
        vm((dp, NZ // NC, 2, half, n), BF16),
        vm((NZ, part, r), F32),
        vm((NZ, part, r), F32),
        vm((NY, part, r), F32),
        vm((dp, NZ, part, r), F32),
        vm((width, r), F32),
        vm((NZ, NY, part, dp * own // NY), F32),
        vm((NY * NZ, part, dp * own // NY), F32),
        vm((NY, part, dp * own // NY), F32),
        vm((dp, NZ, part, r), F32),
        vm((r, 2 * r), F32),
        pltpu.SemaphoreType.DMA((340,)),
        pltpu.SemaphoreType.DMA((340,)),
        pltpu.SemaphoreType.DMA((6,)),
    ]
    flops = 2 * dp * own * n * depth
    results = pl.pallas_call(
        kernel,
        out_shape=(
            jax.ShapeDtypeStruct((width, r), F32),
            jax.ShapeDtypeStruct((r, n), F32),
        ),
        in_specs=[pl.BlockSpec(memory_space=pl.ANY)] * 5,
        out_specs=[pl.BlockSpec(memory_space=pltpu.VMEM)] * 2,
        scratch_shapes=scratch,
        cost_estimate=pl.CostEstimate(
            flops=flops, bytes_accessed=2 * n * depth, transcendentals=own * n
        ),
        compiler_params=pltpu.CompilerParams(
            collective_id=0, has_side_effects=True, vmem_limit_bytes=60 * 1024 * 1024
        ),
    )(out_grad, down_weight, gate_pre, inputs, test_matrix)
    anywhere = pl.BlockSpec(memory_space=pl.ANY)
    return pl.pallas_call(
        hand_over,
        out_shape=tuple(jax.ShapeDtypeStruct(a.shape, a.dtype) for a in results),
        in_specs=[anywhere] * 2,
        out_specs=[anywhere] * 2,
        scratch_shapes=[pltpu.VMEM(a.shape, a.dtype) for a in results]
        + [pltpu.SemaphoreType.DMA((4,))],
    )(*results)


def solution(mesh):
    return jax.shard_map(
        shards,
        mesh=mesh,
        in_specs=(
            P("tensor", "dp"),
            P("tensor", "dp"),
            P("dp", "tensor"),
            P("dp", "tensor"),
            P("tensor", None),
        ),
        out_specs=(P("tensor", None), P(None, "tensor")),
        check_vma=False,
    )
```

```python
import functools
import math

import jax
import jax.numpy as jnp
from jax import lax
from jax.experimental import pallas as pl
from jax.experimental.pallas import tpu as pltpu
from jax.sharding import PartitionSpec as P

MESH = pl.DeviceIdType.MESH
F32 = jnp.float32
BF16 = jnp.bfloat16

NX, NC, NY, NZ = 4, 2, 4, 8
CUT = 1024
LAST = 2 * (NZ // 2) - 1


def slot_from_below(k):
    return LAST if k == NZ // 2 else 2 * k


def slot_from_above(k):
    return LAST if k == NZ // 2 else 2 * k - 1


OFFSET = {0: 0, LAST: NZ // 2}
STEP = {0: 0, LAST: NZ // 2}
for _k in range(1, NZ // 2):
    OFFSET[slot_from_below(_k)] = NZ - _k
    OFFSET[slot_from_above(_k)] = _k
    STEP[slot_from_below(_k)] = STEP[slot_from_above(_k)] = _k

ARRIVALS = [
        (2, 0, 0), (1, 0, 0), (0, 3, 1), (0, 1, 1), (2, 0, 1), (1, 0, 1), (0, 3, 0),
        (0, 1, 0), (0, 2, 1), (4, 0, 0), (3, 0, 0), (2, 3, 0), (2, 1, 0), (2, 3, 1),
        (1, 3, 1), (1, 3, 0), (1, 1, 0), (2, 1, 1), (1, 1, 1), (0, 2, 0), (4, 1, 0),
        (4, 0, 1), (3, 0, 1), (4, 3, 0), (3, 1, 0), (2, 2, 1), (1, 2, 1), (3, 3, 0),
        (1, 2, 0), (6, 0, 0), (5, 0, 0), (2, 2, 0), (4, 3, 1), (3, 3, 1), (4, 2, 0),
        (3, 2, 0), (4, 1, 1), (3, 1, 1), (6, 3, 0), (6, 1, 0), (6, 0, 1), (5, 0, 1),
        (5, 3, 0), (5, 1, 0), (4, 2, 1), (3, 2, 1), (7, 0, 0), (5, 3, 1), (6, 2, 0),
        (6, 3, 1), (5, 1, 1), (5, 2, 0), (6, 1, 1), (5, 2, 1), (7, 3, 0), (7, 1, 0),
        (7, 0, 1), (7, 3, 1), (6, 2, 1), (7, 2, 1), (7, 1, 1), (7, 2, 0),
]
HALF_TURN = {0: True, 1: True, 3: False, 2: False}


def split3(v):
    hi = v.astype(BF16)
    rest = v - hi.astype(F32)
    mid = rest.astype(BF16)
    low = (rest - mid.astype(F32)).astype(BF16)
    return hi, mid, low


def dot(a, b, ca, cb, precision=None):
    return lax.dot_general(
        a, b, (((ca,), (cb,)), ((), ())), preferred_element_type=F32, precision=precision
    )


HIGHEST = lax.Precision.HIGHEST


def inverse_factor(gram, work):
    n = gram.shape[0]
    ri = lax.broadcasted_iota(jnp.int32, (n, n), 0)
    ci = lax.broadcasted_iota(jnp.int32, (n, n), 1)
    work[:, :n] = gram
    work[:, n:] = jnp.where(ri == ci, 1.0, 0.0).astype(F32)
    sub = lax.broadcasted_iota(jnp.int32, (8, n), 0)
    sub2 = lax.broadcasted_iota(jnp.int32, (8, 2 * n), 0)
    for b in range(n // 8):
        rows = slice(8 * b, 8 * b + 8)
        panel = work[rows, :]
        cols = [
            jnp.broadcast_to(panel[:, 8 * b + m : 8 * b + m + 1], (8, n)) for m in range(8)
        ]
        for k in range(8):
            inv = lax.rsqrt(cols[k][k : k + 1, :])
            fac = jnp.where(sub > k, cols[k] * inv, 0.0)
            fac2 = jnp.concatenate([fac, fac], axis=1)
            inv2 = jnp.concatenate([inv, inv], axis=1)
            row = panel[k : k + 1, :] * inv2
            panel = jnp.where(sub2 == k, row, panel - fac2 * row)
            for m in range(k + 1, 8):
                cols[m] = cols[m] - fac * (cols[m][k : k + 1, :] * inv)
        work[rows, :] = panel
        done = 8 * (b + 1)
        if done < n:
            hi = panel.astype(BF16).astype(F32)
            mid = (panel - hi).astype(BF16).astype(F32)
            low = panel - hi - mid
            left = jnp.concatenate([hi, hi, mid, hi, low, mid], axis=0)[:, :n].astype(BF16)
            right = jnp.concatenate([hi, mid, hi, low, hi, mid], axis=0).astype(BF16)
            work[done:, :] = work[done:, :] - dot(left, right, 0, 0)[done:, :]


def kernel(
    og, dw, gate, inp, test, basis, corange,
    GA, GB, W, GT, XB, TM, SIL, PT, SIBR, SIB0, HG, XS, RX, UF,
    SP, S1, S2, SF, RC, KP, KR, KY, TF, WK,
    sends, recvs, local,
):
    d, t = lax.axis_index("dp"), lax.axis_index("tensor")
    x, c = d // NC, lax.rem(d, NC)
    y, z = t // NZ, lax.rem(t, NZ)
    tokens = NX * NC * XB.shape[1]
    factor = 1.0 / math.sqrt(tokens)
    features = inp.shape[1] * NY * NZ

    def mod(a, n):
        return lax.rem(a + n, n)

    def at_yz(yy, zz):
        return {"dp": d, "tensor": yy * NZ + zz}

    def at_xc(xx, cc):
        return {"dp": xx * NC + cc, "tensor": t}

    def around(o, p):
        return {"dp": mod(x + o, NX) * NC + c, "tensor": y * NZ + mod(z + p, NZ)}

    zu, zd = at_yz(y, mod(z + 1, NZ)), at_yz(y, mod(z - 1, NZ))
    yu, yd, y2 = at_yz(mod(y + 1, NY), z), at_yz(mod(y - 1, NY), z), at_yz(mod(y + 2, NY), z)
    xu, xd = mod(x + 1, NX), mod(x - 1, NX)
    twin = at_xc(x, 1 - c)

    pending = []
    count = {"s": 0, "r": 0}

    def finish():
        assert count["s"] <= 340 and count["r"] <= 340, count
        for make, when in pending:
            if when is None:
                make().wait_send()
            else:
                pl.when(when)(make().wait_send)

    def take_recv(n):
        base = count["r"]
        count["r"] += n
        return base

    def send(src, dst, recv, dev, when=None):
        idx = count["s"]
        count["s"] += 1

        def make():
            return pltpu.make_async_remote_copy(
                src_ref=src() if callable(src) else src,
                dst_ref=dst() if callable(dst) else dst,
                send_sem=sends.at[idx], recv_sem=recvs.at[recv() if callable(recv) else recv],
                device_id=dev, device_id_type=MESH,
            )

        if when is None:
            make().start()
        else:
            pl.when(when)(make().start)
        pending.append((make, when))

    def arrive(ref, recv):
        pltpu.make_async_remote_copy(
            src_ref=ref, dst_ref=ref, send_sem=sends.at[0], recv_sem=recvs.at[recv],
            device_id=twin, device_id_type=MESH,
        ).wait_recv()

    q0, qp, qn, q2 = mod(y - x, NY), mod(y - 1 - x, NY), mod(y + 1 - x, NY), mod(y + 2 - x, NY)

    half = og.shape[0] // 2
    loads = [
        pltpu.make_async_copy(og.at[:, pl.ds(0, CUT)], GA.at[q0], local.at[0]),
        pltpu.make_async_copy(
            og.at[:, pl.ds(CUT, og.shape[1] - CUT)], GB.at[q0], local.at[5]
        ),
        pltpu.make_async_copy(inp, XB.at[d], local.at[1]),
        pltpu.make_async_copy(gate, GT, local.at[3]),
        pltpu.make_async_copy(dw, W, local.at[2]),
        pltpu.make_async_copy(test, TM, local.at[4]),
    ]
    for cp in loads:
        cp.start()

    barrier = pltpu.get_barrier_semaphore()
    peers = [zu, zd, yu, yd, y2] + [around(o, 0) for o in range(1, NX)] + [twin]
    for dev in peers:
        pl.semaphore_signal(barrier, inc=1, device_id=dev, device_id_type=MESH)
    pl.semaphore_wait(barrier, len(peers))
    loads[0].wait()
    loads[1].wait()

    ag = take_recv(8 * NY * 2)

    def item(slot, q, h):
        return (GB if h else GA).at[slot * NY + q]

    def mark(slot, q, h):
        return ag + (slot * NY + q) * 2 + h

    def pass_on(slot, q, h, to_slot, dev):
        send(
            lambda: item(slot, q, h), lambda: item(to_slot, q, h),
            lambda: mark(to_slot, q, h), dev
        )

    def got(slot, q, h):
        arrive(item(slot, q, h), mark(slot, q, h))

    below, above = slot_from_below, slot_from_above
    TOP = NZ // 2

    pass_on(0, q0, 0, below(1), zu)
    pass_on(0, q0, 0, above(1), zd)
    pass_on(0, q0, 1, 0, yu)
    pass_on(0, q0, 1, 0, yd)
    pass_on(0, q0, 1, below(1), zu)
    pass_on(0, q0, 1, above(1), zd)
    pass_on(0, q0, 0, 0, yu)
    pass_on(0, q0, 0, 0, yd)
    pass_on(0, q0, 1, 0, y2)

    loads[2].wait()
    xr = take_recv(NX * NC)
    for o in (1, 3, 2):
        send(XB.at[d], XB.at[d], xr + d, at_xc(mod(x + o, NX), c))
    send(XB.at[d], XB.at[d], xr + d, twin)

    row = [q0, qn, q2, qp]

    def arrival(slot, b, h):
        q, k, up = row[b], STEP[slot], slot % 2 == 0
        got(slot, q, h)
        if h:
            if slot == 0:
                pass_on(0, q, 1, below(1), zu)
                pass_on(0, q, 1, above(1), zd)
            elif slot != LAST and (k + 1 < TOP or HALF_TURN[b] == up):
                if up:
                    pass_on(slot, q, 1, below(k + 1), zu)
                else:
                    pass_on(slot, q, 1, above(k + 1), zd)
        elif b == 0:
            if slot != LAST:
                if up:
                    pass_on(slot, q, 0, below(k + 1), zu)
                elif k + 1 < TOP:
                    pass_on(slot, q, 0, above(k + 1), zd)
            pass_on(slot, q, 0, slot, yu)
            pass_on(slot, q, 0, slot, yd)
        elif b == 3 and up:
            pass_on(slot, q, 0, slot, yu)
        elif b == 1 and not up:
            pass_on(slot, q, 0, slot, yd)

    sibs = take_recv(NZ)
    sib0 = take_recv(NZ // NC * 2)
    rx = take_recv(3 * (NZ // NC) * 2)
    n = W.shape[0]
    WIDE = 256

    def column(s):
        return lax.rem(z + OFFSET[s], NZ)

    def owner_of(s):
        return column(s) // (NZ // NC), lax.rem(column(s), NZ // NC)

    def product(s0, slots, events):
        rows = slots * NY * 2 * half

        def cols_at(start, width):
            blocks = pl.ds(s0 * NY, slots * NY)
            a = jnp.concatenate(
                [g[blocks].reshape(rows, g.shape[2]) for g in (GA, GB)], axis=1
            )
            b = W[pl.ds(start, width), :]
            v = dot(a, b, 1, 1).reshape(slots, NY, 2, half, width)
            for h in range(2):
                PT[pl.ds(s0, slots), h, :, :, pl.ds(start, width)] = v[:, :, h]

        def body(j, _):
            cols_at(pl.multiple_of(j * WIDE, WIDE), WIDE)
            for i, todo in enumerate(events):
                if todo:

                    @pl.when(j == i)
                    def _():
                        for act in todo:
                            act()

            return 0

        assert len(events) <= n // WIDE
        lax.fori_loop(0, n // WIDE, body, 0)
        if n % WIDE:
            cols_at(n - n % WIDE, n % WIDE)

    def exchange(s):
        core, zc = owner_of(s)
        send(
            lambda: PT.at[s, 1 - c, pl.ds(1, NX - 1)], lambda: SIBR.at[s], sibs + s, twin
        )
        for h in range(2):
            send(
                lambda h=h: PT.at[s, h, 0], lambda h=h: SIB0.at[zc, h], sib0 + zc * 2 + h,
                twin, core != c,
            )

        @pl.when(core == c)
        def _():
            HG[zc] = PT[s, :, 0]

    owners = [owner_of(s) for s in range(NZ)]
    targets = [[at_xc(mod(x + o, NX), owners[s][0]) for o in range(1, NX)] for s in range(NZ)]
    marks = [
        [rx + ((o - 1) * (NZ // NC) + owners[s][1]) * 2 + c for o in range(1, NX)]
        for s in range(NZ)
    ]

    def outward(s):
        zc = owners[s][1]
        arrive(SIBR.at[s], sibs + s)
        XS[s] = (PT[s, c, 1:] + SIBR[s]).astype(BF16)
        for o in (2, 1, 3):
            send(
                lambda o=o: XS.at[s, o - 1], lambda o=o: RX.at[o - 1, zc, c],
                marks[s][o - 1], targets[s][o - 1],
            )

    def own(s):
        core, zc = owners[s]

        @pl.when(core == c)
        def _():
            for h in range(2):
                arrive(SIB0.at[zc, h], sib0 + zc * 2 + h)
            v = HG[zc] + SIB0[zc]
            for o in range(1, NX):
                for h in range(2):
                    arrive(
                        RX.at[o - 1, zc, h], rx + ((o - 1) * (NZ // NC) + zc) * 2 + h
                    )
                v = v + RX[o - 1, zc].astype(F32)
            UF[d, zc] = (v * SIL[zc].reshape(2, half, n)).astype(BF16)

    groups = [[0]] + [[above(k), below(k)] for k in range(1, TOP)] + [[LAST]]
    ur, tr = take_recv(NX * NC * (NZ // NC)), take_recv(NX * NC)
    same_core = [at_xc(mod(x + o, NX), c) for o in range(NX)]
    mine = [owners[s][0] == c for s in range(NZ)]
    row_marks = [ur + d * (NZ // NC) + owners[s][1] for s in range(NZ)]

    def rows_out(s):
        core, zc = owners[s]
        for o in (2, 1, 3):
            send(
                lambda: UF.at[d, zc], lambda: UF.at[d, zc], row_marks[s], same_core[o], mine[s]
            )

    ends = [
        1 + max(i for i, a in enumerate(ARRIVALS) if a[0] in g) for g in groups
    ]

    def to_other_core():
        for o in (1, 3, 2):
            e = mod(x + o, NX) * NC + c
            arrive(XB.at[e], xr + e)
            send(XB.at[e], XB.at[e], xr + e, twin)

    def inner_terms():
        rows, width = XB.shape[1], XB.shape[2]
        for o in range(NX):
            e = mod(x + o, NX) * NC + 1 - c
            arrive(XB.at[e], xr + e)
        v = dot(XB[d], XB[...].reshape(NX * NC * rows, width), 1, 1)
        part, wide = KP.shape[2], KP.shape[3]
        for zz in range(NZ):
            for yy in range(NY):
                KP[zz, yy] = v[
                    zz * part : (zz + 1) * part, yy * wide : (yy + 1) * wide
                ]

    kr, ky = take_recv(NY * NZ), take_recv(NY)
    hops = [(o, p) for p in (4, 3, 5, 2, 6, 1, 7, 0) for o in (2, 1, 3, 0) if o or p]

    def inner_out():
        for o, p in hops:
            yy, zz = mod(y + o, NY), mod(z + p, NZ)
            send(KP.at[zz, yy], KR.at[t], kr + t, at_yz(yy, zz))
        KR[t] = KP[z, y]

    def inner_sum():
        for o, p in hops[::-1]:
            tt = mod(y + o, NY) * NZ + mod(z + p, NZ)
            arrive(KR.at[tt], kr + tt)
        v = KR[0]
        for j in range(1, NY * NZ):
            v = v + KR[j]
        KY[y] = v
        for o in (2, 1, 3):
            send(KY.at[y], KY.at[y], ky + y, at_yz(mod(y + o, NY), z))

    def inner_rows():
        for o in (1, 3, 2):
            yy = mod(y + o, NY)
            arrive(KY.at[yy], ky + yy)
        return jnp.concatenate([KY[j] for j in range(NY)], axis=1)

    loads[3].wait()
    g = GT[...].astype(F32)
    SIL[...] = (g * (1.0 / (1.0 + jnp.exp(-g)))).reshape(SIL.shape)
    for a in ARRIVALS[: ends[0]]:
        arrival(*a)
    loads[4].wait()
    turns = n // WIDE
    for k in range(TOP + 1):
        todo = ARRIVALS[ends[k] : ends[k + 1]] if k < TOP else []
        each = max(2, -(-len(todo) // turns))
        events = [
            [functools.partial(arrival, *a) for a in todo[i * each : (i + 1) * each]]
            for i in range(turns)
        ]
        if k >= 1:
            events[3] += [functools.partial(outward, s) for s in groups[k - 1]]
        if k == TOP:
            for s in groups[0] + groups[1]:
                events[5] += [functools.partial(own, s), functools.partial(rows_out, s)]
        if k == TOP:
            inner_out()
        product(groups[k][0], len(groups[k]), events)
        for s in groups[k]:
            exchange(s)
        if k == 2:
            to_other_core()
        if k == 3:
            inner_terms()
    outward(LAST)
    loads[5].wait()
    for s in groups[TOP - 2] + groups[TOP - 1] + groups[TOP]:
        own(s)
    for k in range(TOP - 2, TOP + 1):
        for s in groups[k]:
            rows_out(s)
    send(UF.at[d], UF.at[d], tr + d, twin)

    def up_grad_to_twin():
        for o in (1, 3, 2):
            e = mod(x + o, NX) * NC + c
            for zc in range(NZ // NC):
                arrive(UF.at[e, zc], ur + e * (NZ // NC) + zc)
            send(UF.at[e], UF.at[e], tr + e, twin)

    def up_grad_from_twin():
        for o in range(NX):
            e = mod(x + o, NX) * NC + 1 - c
            arrive(UF.at[e], tr + e)

    r = TM.shape[1]
    part = r // NZ
    rows_own = XB.shape[1]

    def summed(src, first, second, between):
        r1, r2 = take_recv(NZ), take_recv(NY)
        first[z] = src[z]
        for o in (4, 3, 5, 2, 6, 1, 7):
            zz = mod(z + o, NZ)
            send(src.at[zz], first.at[z], r1 + z, at_yz(y, zz))
        for o in (1, 7, 2, 6, 3, 5, 4):
            zz = mod(z + o, NZ)
            arrive(first.at[zz], r1 + zz)
        v = first[0]
        for j in range(1, NZ):
            v = v + first[j]
        second[y] = v
        for o in (2, 1, 3):
            send(second.at[y], second.at[y], r2 + y, at_yz(mod(y + o, NY), z))
        between()
        for o in (1, 3, 2):
            yy = mod(y + o, NY)
            arrive(second.at[yy], r2 + yy)
        v = second[0]
        for j in range(1, NY):
            v = v + second[j]
        return v

    pairs = [(o, p) for o in (2, 1, 3, 0) for p in (4, 3, 5, 2, 6, 1, 7, 0) if o or p]

    def spread(full):
        base = take_recv(NX * NZ)
        for o, p in pairs:
            send(full.at[d, z], full.at[d, z], base + x * NZ + z, around(o, p))
        return base

    def collect(full, base):
        other = take_recv(NX)
        for o in (0, 1, 3, 2):
            xx = mod(x + o, NX)
            for p in (0, 1, 7, 2, 6, 3, 5, 4):
                if o or p:
                    zz = mod(z + p, NZ)
                    arrive(full.at[xx * NC + c, zz], base + xx * NZ + zz)
            send(full.at[xx * NC + c], full.at[xx * NC + c], other + xx, twin)
        return other

    def from_twin(full, other):
        for o in (0, 1, 3, 2):
            xx = mod(x + o, NX)
            arrive(full.at[xx * NC + 1 - c], other + xx)

    u = UF[d].reshape(rows_own, n)
    SP[...] = dot(u, TM[...], 1, 0).reshape(NZ, part, r)
    v = summed(SP, S1, S2, inner_sum)
    SF[d, z] = v
    base = spread(SF)
    inner = inner_rows()
    other = collect(SF, base)
    from_twin(SF, other)

    s = SF[...].reshape(tokens, r)
    TF[d, z] = dot(inner, s, 1, 0, HIGHEST) * factor
    base = spread(TF)

    every = XB[...].reshape(tokens, XB.shape[2])
    rc = dot(every, jnp.concatenate(split3(s), axis=1), 0, 0)
    RC[...] = (rc[:, :r] + (rc[:, r : 2 * r] + rc[:, 2 * r :])) * factor
    up_grad_to_twin()
    from_twin(TF, collect(TF, base))
    tt = TF[...].reshape(tokens, r)
    inverse_factor(dot(SF[...].reshape(tokens, r), tt, 0, 0, HIGHEST) * factor, WK)
    inv = WK[:, r:]
    basis[...] = dot(RC[...], inv, 1, 1, HIGHEST) * math.sqrt(features)
    up_grad_from_twin()
    cot = dot(inv, tt, 1, 1, HIGHEST) * factor
    hi = cot.astype(BF16)
    low = (cot - hi.astype(F32)).astype(BF16)
    both = dot(jnp.concatenate([hi, low], axis=0), UF[...].reshape(tokens, n), 1, 0)
    corange[...] = both[:r] + both[r:]
    finish()


def hand_over(basis_in, corange_in, basis, corange, basis_held, corange_held, done):
    into = [
        pltpu.make_async_copy(basis_in, basis_held, done.at[0]),
        pltpu.make_async_copy(corange_in, corange_held, done.at[1]),
    ]
    out = [
        pltpu.make_async_copy(basis_held, basis, done.at[2]),
        pltpu.make_async_copy(corange_held, corange, done.at[3]),
    ]
    for cp in into:
        cp.start()
    for first, second in zip(into, out):
        first.wait()
        second.start()
    for cp in out:
        cp.wait()


def shards(out_grad, down_weight, gate_pre, inputs, test_matrix):
    rows, depth = out_grad.shape
    n = down_weight.shape[0]
    own, width = inputs.shape
    r = test_matrix.shape[1]
    half = rows // 2
    part = r // NZ
    dp = NX * NC
    vm = pltpu.VMEM
    scratch = [
        vm((NZ * NY, rows, CUT), BF16),
        vm((NZ * NY, rows, depth - CUT), BF16),
        vm((n, depth), BF16),
        vm((own, n), BF16),
        vm((dp, own, width), BF16),
        vm((n, r), BF16),
        vm((NZ // NC, rows, n), F32),
        vm((NZ, 2, NY, half, n), F32),
        vm((NZ, NX - 1, half, n), F32),
        vm((NZ // NC, 2, half, n), F32),
        vm((NZ // NC, 2, half, n), F32),
        vm((NZ, NX - 1, half, n), BF16),
        vm((NX - 1, NZ // NC, 2, half, n), BF16),
        vm((dp, NZ // NC, 2, half, n), BF16),
        vm((NZ, part, r), F32),
        vm((NZ, part, r), F32),
        vm((NY, part, r), F32),
        vm((dp, NZ, part, r), F32),
        vm((width, r), F32),
        vm((NZ, NY, part, dp * own // NY), F32),
        vm((NY * NZ, part, dp * own // NY), F32),
        vm((NY, part, dp * own // NY), F32),
        vm((dp, NZ, part, r), F32),
        vm((r, 2 * r), F32),
        pltpu.SemaphoreType.DMA((340,)),
        pltpu.SemaphoreType.DMA((340,)),
        pltpu.SemaphoreType.DMA((6,)),
    ]
    flops = 2 * dp * own * n * depth
    results = pl.pallas_call(
        kernel,
        out_shape=(
            jax.ShapeDtypeStruct((width, r), F32),
            jax.ShapeDtypeStruct((r, n), F32),
        ),
        in_specs=[pl.BlockSpec(memory_space=pl.ANY)] * 5,
        out_specs=[pl.BlockSpec(memory_space=pltpu.VMEM)] * 2,
        scratch_shapes=scratch,
        cost_estimate=pl.CostEstimate(
            flops=flops, bytes_accessed=2 * n * depth, transcendentals=own * n
        ),
        compiler_params=pltpu.CompilerParams(
            collective_id=0, has_side_effects=True, vmem_limit_bytes=60 * 1024 * 1024
        ),
    )(out_grad, down_weight, gate_pre, inputs, test_matrix)
    anywhere = pl.BlockSpec(memory_space=pl.ANY)
    return pl.pallas_call(
        hand_over,
        out_shape=tuple(jax.ShapeDtypeStruct(a.shape, a.dtype) for a in results),
        in_specs=[anywhere] * 2,
        out_specs=[anywhere] * 2,
        scratch_shapes=[pltpu.VMEM(a.shape, a.dtype) for a in results]
        + [pltpu.SemaphoreType.DMA((4,))],
    )(*results)


def solution(mesh):
    return jax.shard_map(
        shards,
        mesh=mesh,
        in_specs=(
            P("tensor", "dp"),
            P("tensor", "dp"),
            P("dp", "tensor"),
            P("dp", "tensor"),
            P("tensor", None),
        ),
        out_specs=(P("tensor", None), P(None, "tensor")),
        check_vma=False,
    )
```
